256 devices in a mesh: row: 16 (over z, y_lo), col: 16 (over y_hi, x, core).
Axes of the slice: x: 4, y: 4 (y_hi: 2, y_lo: 2; y = y_hi * 2 + y_lo), z: 8, core: 2. Of those that a mesh axis runs over, the one named last changes fastest.
Arguments:
- pair_rep: bfloat16 [1024, 1024, 128], P('row', 'col'), may hold values from -6 to 6
- in_gain: float32 [128], replicated, may hold values from 0.5 to 1.5
- proj_weight: bfloat16 [128, 512], replicated, may hold values from -0.5 to 0.5
- gate_weight: bfloat16 [128, 128], replicated, may hold values from -0.5 to 0.5
- out_gain: float32 [128], replicated, may hold values from 0.5 to 1.5
- out_weight: bfloat16 [128, 128], replicated, may hold values from -0.5 to 0.5
Outputs:
- update: bfloat16 [1024, 1024, 128], P('row', 'col')
The draws below stay inside these ranges and needn't reach their ends.
All inputs are finite; a program needn't handle non-finite values.
Results may differ from the reference program's by a relative error of at most 0.0078.
Values may be sent and summed in bfloat16 or wider, within the bound.
A program may use at most 192 MiB of HBM per device.

```python
import jax
import jax.numpy as jnp
from jax import lax

PAIR_WIDTH = 128
HIDDEN_SIZE = 128
RESIDUES = 1024


def block_levels(own_key, dims, cuts, smallest, top_value):
    loudness = 1.0
    for position, parts in cuts:
        draws = jax.random.uniform(jax.random.fold_in(jax.random.fold_in(own_key, 6), position), (parts,), jnp.float32, smallest / len(cuts), top_value / len(cuts))
        loudness = loudness * jnp.repeat(jnp.exp(draws), dims[position] // parts).reshape((-1,) + (1,) * (len(dims) - 1 - position))
    return loudness


def normal_values(key, dims, spread, limit, cuts=(), held_as=jnp.bfloat16):
    level = block_levels(key, dims, cuts, -0.22, 0.18) if cuts else 1.0
    array = jax.random.normal(key, dims, jnp.float32) * spread * level
    return jnp.minimum(jnp.maximum(array, -limit), limit).astype(held_as)


def setup_inputs(seed: int = 0) -> dict:
    key_of = jax.random.split(jax.random.key(seed), 7)
    pair_rep = normal_values(key_of[0], (RESIDUES, RESIDUES, PAIR_WIDTH), 1.0, 6.0, ((0, 16), (1, 16)))
    in_gain = jnp.clip(1.0 + 0.1 * jax.random.normal(key_of[1], (PAIR_WIDTH,), jnp.float32), 0.5, 1.5)
    proj_weight = normal_values(key_of[2], (PAIR_WIDTH, 4 * HIDDEN_SIZE), PAIR_WIDTH ** -0.5, 0.5)
    gate_weight = normal_values(key_of[3], (PAIR_WIDTH, PAIR_WIDTH), PAIR_WIDTH ** -0.5, 0.5)
    out_gain = jnp.clip(1.0 + 0.1 * jax.random.normal(key_of[4], (HIDDEN_SIZE,), jnp.float32), 0.5, 1.5)
    out_weight = normal_values(key_of[5], (HIDDEN_SIZE, PAIR_WIDTH), HIDDEN_SIZE ** -0.5, 0.5)
    return {"pair_rep": pair_rep, "in_gain": in_gain, "proj_weight": proj_weight, "gate_weight": gate_weight, "out_gain": out_gain, "out_weight": out_weight}


EPSILON = 1e-05

def layer_norm(values, gain_vec):
    chan_mean = lax.optimization_barrier(jnp.mean(values, axis=-1, keepdims=True))
    centred = values - chan_mean
    chan_var = lax.optimization_barrier(jnp.mean(centred * centred, axis=-1, keepdims=True))
    return centred * lax.rsqrt(chan_var + EPSILON) * gain_vec

def reference(pair_rep, in_gain, proj_weight, gate_weight, out_gain, out_weight):
    hidden = out_weight.shape[0]
    normed = layer_norm(pair_rep.astype(jnp.float32), in_gain).astype(jnp.bfloat16)
    projected = jnp.dot(normed, proj_weight, preferred_element_type=jnp.float32)
    left_side = (jax.nn.sigmoid(projected[..., hidden:2 * hidden]) * projected[..., :hidden]).astype(jnp.bfloat16)
    right_side = (jax.nn.sigmoid(projected[..., 3 * hidden:]) * projected[..., 2 * hidden:3 * hidden]).astype(jnp.bfloat16)
    tri_sum = jnp.einsum('ikh,jkh->ijh', left_side.astype(jnp.float32), right_side.astype(jnp.float32))
    tri_normed = layer_norm(tri_sum, out_gain).astype(jnp.bfloat16)
    gate = jax.nn.sigmoid(jnp.dot(normed, gate_weight, preferred_element_type=jnp.float32))
    return (gate * jnp.dot(tri_normed, out_weight, preferred_element_type=jnp.float32)).astype(jnp.bfloat16)
```

```python
import functools

import jax
import jax.numpy as jnp
from jax import lax
from jax.experimental import pallas as pl
from jax.experimental.pallas import tpu as pltpu
from jax.sharding import PartitionSpec as P

EPSILON = 1e-05
MESH = pl.DeviceIdType.MESH
F32, BF16 = jnp.float32, jnp.bfloat16

CHUNKS = 2
ROWS = 32 // CHUNKS
NT = (((1,), (1,)), ((), ()))
TN = (((0,), (0,)), ((), ()))


def sigmoid(values):
    return 0.5 * jnp.tanh(0.5 * values) + 0.5


def kernel(
    x_ref, in_gain_ref, proj_ref, gate_w_ref, out_gain_ref, out_w_ref, o_ref,
    normed, other, wide, right_send, left_send, right_buf, left_buf,
    tri_send, tri_buf, gates, result, weights_t, gain_cols,
    ready, swap_sems, right_sems, fwd_sems, left_sems, tri_sems, out_sems, local_sems,
):
    row, col = lax.axis_index("row"), lax.axis_index("col")
    z, y_lo = row // 2, lax.rem(row, 2)
    pair, core = col // 2, lax.rem(col, 2)
    y_hi, x = pair // 4, lax.rem(pair, 4)
    me = row * 8 + pair
    sibling = (row, pair * 2 + 1 - core)

    def shifted(dz, dyl, dyh, dx):
        row2 = lax.rem(z + dz, 8) * 2 + lax.rem(y_lo + dyl, 2)
        pair2 = lax.rem(y_hi + dyh, 2) * 4 + lax.rem(x + dx, 4)
        return row2, pair2

    def shifted_all(step):
        dz, rest = lax.rem(step, 8), step // 8
        return shifted(dz, lax.rem(rest // 4, 2), rest // 8, lax.rem(rest, 4))

    barrier = pltpu.get_barrier_semaphore()

    def greet(device):
        pl.semaphore_signal(barrier, inc=1, device_id=device, device_id_type=MESH)

    def greet_z(step, carry):
        row2, pair2 = shifted(step, 0, 0, 0)
        greet((row2, pair2 * 2 + core))
        return carry

    def greet_plane(step, carry):
        row2, pair2 = shifted(0, lax.rem(step // 4, 2), step // 8, lax.rem(step, 4))
        greet((row2, pair2 * 2 + core))
        return carry

    greet(sibling)
    lax.fori_loop(1, 16, greet_plane, 0)
    lax.fori_loop(1, 8, greet_z, 0)

    gain = in_gain_ref[...]

    def norm_rows(values):
        values = values.astype(F32).reshape(-1, 128)
        mean = jnp.mean(values, axis=-1, keepdims=True)
        centred = values - mean
        var = jnp.mean(centred * centred, axis=-1, keepdims=True)
        return (centred * lax.rsqrt(var + EPSILON) * gain).astype(BF16)

    def norm_away(step, carry):
        first = pl.multiple_of(step * 4, 4)
        other[pl.ds(first, 4)] = norm_rows(x_ref[pl.ds(32 * (1 - core) + first, 4)]).reshape(4, 64, 128)
        return carry

    def norm_own(step, carry):
        first = pl.multiple_of(step * 4, 4)
        normed[pl.ds(first, 4), pl.ds(pl.multiple_of(64 * core, 64), 64), :] = norm_rows(
            x_ref[pl.ds(32 * core + first, 4)]
        ).reshape(4, 64, 128)
        return carry

    lax.fori_loop(0, 8, norm_away, 0)
    pl.semaphore_wait(barrier, 23)
    swap = pltpu.make_async_remote_copy(
        src_ref=other,
        dst_ref=normed.at[:, pl.ds(pl.multiple_of(64 * core, 64), 64), :],
        send_sem=swap_sems.at[0], recv_sem=swap_sems.at[1],
        device_id=sibling, device_id_type=MESH,
    )
    swap.start()

    def ready_z(step, carry):
        row2, pair2 = shifted(step, 0, 0, 0)
        pl.semaphore_signal(
            ready, inc=1, device_id=(row2, pair2 * 2 + core), device_id_type=MESH
        )
        return carry

    lax.fori_loop(1, 8, ready_z, 0)
    lax.fori_loop(0, 8, norm_own, 0)
    weights_t[...] = proj_ref[...].astype(F32).T.astype(BF16)
    gain_cols[...] = jnp.broadcast_to(out_gain_ref[...], (128, 128)).T
    swap.wait()

    def project(first_row, send, chunks):
        half = weights_t[first_row : first_row + 256, :]

        def some(step, carry):
            first = pl.multiple_of(step * 4, 4)
            rows = normed[pl.ds(first, 4)].reshape(512, 128)
            both = lax.dot_general(half, rows, NT, preferred_element_type=F32)
            side = sigmoid(both[128:]) * both[:128]
            for i in range(4):
                wide[pl.ds(first + i, 128, stride=32), :] = side[:, i * 128 : (i + 1) * 128]
            return carry

        lax.fori_loop(0, 8, some, 0)
        size = 32 // chunks

        def narrow(step, carry):
            block = wide[pl.ds(pl.multiple_of(step * 128, 128), 128), :].astype(BF16)
            block = block.reshape(4, chunks, size, 128)
            for c in range(chunks):
                send[c, pl.ds(step * 4, 4)] = block[:, c]
            return carry

        lax.fori_loop(0, 32, narrow, 0)

    project(256, right_send, 1)
    pl.semaphore_wait(ready, 7)

    def send_right(step, carry):
        row2, pair2 = shifted_all(step)
        pltpu.make_async_remote_copy(
            src_ref=right_send.at[0, row2 * 8 + pair2],
            dst_ref=right_buf.at[row, core, pair],
            send_sem=right_sems.at[0], recv_sem=right_sems.at[1],
            device_id=(row2, pair2 * 2 + core), device_id_type=MESH,
        ).start()
        return carry

    lax.fori_loop(1, 128, send_right, 0)
    own_right = pltpu.make_async_copy(
        right_send.at[0, me], right_buf.at[row, core, pair], local_sems.at[0]
    )
    own_right.start()

    project(0, left_send, CHUNKS)
    own_left = []
    for c in range(CHUNKS):

        def send_left(step, carry, c=c):
            row2, pair2 = shifted_all(step)
            pltpu.make_async_remote_copy(
                src_ref=left_send.at[c, row2 * 8 + pair2],
                dst_ref=left_buf.at[c, row, pair],
                send_sem=left_sems.at[0, c], recv_sem=left_sems.at[1, c],
                device_id=(row2, pair2 * 2 + core), device_id_type=MESH,
            ).start()
            return carry

        lax.fori_loop(1, 128, send_left, 0)
        own = pltpu.make_async_copy(
            left_send.at[c, me], left_buf.at[c, row, pair], local_sems.at[1 + c]
        )
        own.start()
        own_left.append(own)

    def gate_rows(step, carry):
        first = pl.multiple_of(step * 4, 4)
        rows = normed[pl.ds(first, 4)].reshape(512, 128)
        gates[pl.ds(first, 4)] = sigmoid(
            jnp.dot(rows, gate_w_ref[...], preferred_element_type=F32)
        ).reshape(4, 128, 128)
        return carry

    lax.fori_loop(0, 8, gate_rows, 0)

    def wait_all(refs, sems):
        copy = pltpu.make_async_remote_copy(
            src_ref=refs.at[pl.ds(0, 127)], dst_ref=refs.at[pl.ds(0, 127)],
            send_sem=sems[0], recv_sem=sems[1], device_id=sibling, device_id_type=MESH,
        )
        return copy

    own_right.wait()
    wait_all(right_send.at[0], (right_sems.at[0], right_sems.at[1])).wait_recv()
    forward = pltpu.make_async_remote_copy(
        src_ref=right_buf.at[:, core], dst_ref=right_buf.at[:, core],
        send_sem=fwd_sems.at[0], recv_sem=fwd_sems.at[1],
        device_id=sibling, device_id_type=MESH,
    )
    forward.start()
    forward.wait()

    for c in range(CHUNKS):
        own_left[c].wait()
        wait_all(left_send.at[c], (left_sems.at[0, c], left_sems.at[1, c])).wait_recv()

        def columns(step, carry, c=c):
            n = lax.rem(step + pair // 2, 4)
            total = None
            for k in range(4):
                left = jnp.concatenate(
                    [left_buf[c, :, 2 * k + s].reshape(16 * ROWS, 128) for s in range(2)], axis=-1
                )
                right = jnp.concatenate(
                    [right_buf[pl.ds(4 * n, 4), :, 2 * k + s].reshape(256, 128) for s in range(2)],
                    axis=-1,
                )
                term = lax.dot_general(left, right, NT, preferred_element_type=F32)
                total = term if total is None else total + term
            tiles = total.astype(BF16).reshape(16, ROWS, 256)
            for s in range(2):
                tri_send[c, :, 2 * n + s] = tiles[:, :, s * 128 : (s + 1) * 128]

            def send_tri(part, inner):
                dz, rest = lax.rem(part, 8), part // 8
                row2 = lax.rem(z + dz, 8) * 2 + lax.rem(y_lo + rest // 2, 2)
                pair2 = 2 * n + lax.rem(pair + lax.rem(rest, 2), 2)
                away = row2 * 8 + pair2 != me

                @pl.when(away)
                def _():
                    pltpu.make_async_remote_copy(
                        src_ref=tri_send.at[c, row2, pair2],
                        dst_ref=tri_buf.at[c, me],
                        send_sem=tri_sems.at[0, c], recv_sem=tri_sems.at[1, c],
                        device_id=(row2, pair2 * 2 + core), device_id_type=MESH,
                    ).start()

                return inner

            lax.fori_loop(0, 32, send_tri, 0)
            return carry

        lax.fori_loop(0, 4, columns, 0)
        own = pltpu.make_async_copy(
            tri_send.at[c, row, pair], tri_buf.at[c, me], local_sems.at[1 + CHUNKS + c]
        )
        own.start()
        own.wait()

    for c in range(CHUNKS):
        wait_all(left_send.at[c], (tri_sems.at[0, c], tri_sems.at[1, c])).wait_recv()

        def channel_sum(first, size):
            def add(h, acc):
                return acc + tri_buf[c, h].astype(F32)

            return lax.fori_loop(0, 128, add, jnp.zeros((ROWS, 128), F32), unroll=8)

        mean = channel_sum(0, 128) * (1.0 / 128.0)

        def add_square(h, acc, c=c, mean=mean):
            centred = tri_buf[c, h].astype(F32) - mean
            wide[pl.ds(pl.multiple_of(h * ROWS, ROWS), ROWS), :] = centred
            return acc + centred * centred

        var = lax.fori_loop(0, 128, add_square, jnp.zeros((ROWS, 128), F32), unroll=8) * (1.0 / 128.0)
        scale = lax.rsqrt(var + EPSILON)
        scales = gain_cols[...]
        for i in range(ROWS):
            tile = wide[pl.ds(i, 128, stride=ROWS), :] * scale[i : i + 1, :] * scales
            projected = lax.dot_general(
                tile.astype(BF16), out_w_ref[...], TN, preferred_element_type=F32
            )
            result[c * ROWS + i] = (gates[c * ROWS + i] * projected).astype(BF16)

    keep = pltpu.make_async_copy(
        result.at[:, pl.ds(pl.multiple_of(64 * core, 64), 64), :],
        o_ref.at[pl.ds(32 * core, 32)], local_sems.at[1 + 2 * CHUNKS],
    )
    keep.start()
    give = pltpu.make_async_remote_copy(
        src_ref=result.at[:, pl.ds(pl.multiple_of(64 * (1 - core), 64), 64), :],
        dst_ref=o_ref.at[pl.ds(32 * core, 32)],
        send_sem=out_sems.at[0], recv_sem=out_sems.at[1],
        device_id=sibling, device_id_type=MESH,
    )
    give.start()
    wait_all(right_send.at[0], (right_sems.at[0], right_sems.at[1])).wait_send()
    for c in range(CHUNKS):
        wait_all(left_send.at[c], (left_sems.at[0, c], left_sems.at[1, c])).wait_send()
        wait_all(left_send.at[c], (tri_sems.at[0, c], tri_sems.at[1, c])).wait_send()
    keep.wait()
    give.wait()


def shards(pair_rep, in_gain, proj_weight, gate_weight, out_gain, out_weight):
    vmem = pl.BlockSpec(memory_space=pltpu.VMEM)
    return pl.pallas_call(
        kernel,
        out_shape=jax.ShapeDtypeStruct((64, 64, 128), BF16),
        in_specs=[vmem] * 6,
        out_specs=pl.BlockSpec(memory_space=pl.ANY),
        scratch_shapes=[
            pltpu.VMEM((32, 128, 128), BF16),
            pltpu.VMEM((32, 64, 128), BF16),
            pltpu.VMEM((128 * 32, 128), F32),
            pltpu.VMEM((1, 128, 32, 128), BF16),
            pltpu.VMEM((CHUNKS, 128, ROWS, 128), BF16),
            pltpu.VMEM((16, 2, 8, 32, 128), BF16),
            pltpu.VMEM((CHUNKS, 16, 8, ROWS, 128), BF16),
            pltpu.VMEM((CHUNKS, 16, 8, ROWS, 128), BF16),
            pltpu.VMEM((CHUNKS, 128, ROWS, 128), BF16),
            pltpu.VMEM((32, 128, 128), F32),
            pltpu.VMEM((32, 128, 128), BF16),
            pltpu.VMEM((512, 128), BF16),
            pltpu.VMEM((128, 128), F32),
            pltpu.SemaphoreType.REGULAR,
            pltpu.SemaphoreType.DMA((2,)),
            pltpu.SemaphoreType.DMA((2,)),
            pltpu.SemaphoreType.DMA((2,)),
            pltpu.SemaphoreType.DMA((2, CHUNKS)),
            pltpu.SemaphoreType.DMA((2, CHUNKS)),
            pltpu.SemaphoreType.DMA((2,)),
            pltpu.SemaphoreType.DMA((2 + 2 * CHUNKS,)),
        ],
        compiler_params=pltpu.CompilerParams(
            collective_id=0, has_side_effects=True, vmem_limit_bytes=40 * 2**20
        ),
    )(
        pair_rep, in_gain.reshape(1, 128), proj_weight, gate_weight,
        out_gain.reshape(1, 128), out_weight,
    )


def solution(mesh):
    return jax.shard_map(
        shards,
        mesh=mesh,
        in_specs=(P("row", "col", None), P(), P(), P(), P(), P()),
        out_specs=P("row", "col", None),
        check_vma=False,
    )
```

```python
import jax
import jax.numpy as jnp
from jax import lax
from jax.experimental import pallas as pl
from jax.experimental.pallas import tpu as pltpu
from jax.sharding import PartitionSpec as P

EPSILON = 1e-05
MESH = pl.DeviceIdType.MESH
F32, BF16 = jnp.float32, jnp.bfloat16

CHUNKS = 2
ROWS = 32 // CHUNKS
NT = (((1,), (1,)), ((), ()))
TN = (((0,), (0,)), ((), ()))


def sigmoid(values):
    return 0.5 * jnp.tanh(0.5 * values) + 0.5


def kernel(
    x_hbm, in_gain_hbm, proj_hbm, gate_w_hbm, out_gain_hbm, out_w_hbm, o_ref,
    x_ref, in_gain_ref, proj_ref, gate_w_ref, out_gain_ref, out_w_ref,
    normed, other, wide, right_send, left_send, right_buf, left_buf,
    tri_send, tri_buf, gates, result, weights_t, gain_cols,
    ready, ready_core, load_sems, swap_sems, right_sems, own_sems, fwd_sems,
    left_sems, tri_sems, out_sems,
):
    row, col = lax.axis_index("row"), lax.axis_index("col")
    z, y_lo = row // 2, lax.rem(row, 2)
    pair, core = col // 2, lax.rem(col, 2)
    y_hi, x = pair // 4, lax.rem(pair, 4)
    place = y_lo * 8 + pair
    up = 1 - core
    me = lax.rem(z + 8 - core, 8) * 16 + place
    sibling = (row, pair * 2 + 1 - core)
    partner = (lax.rem(z + 7 + 2 * up, 8) * 2 + y_lo, pair * 2 + 1 - core)

    loads = [
        pltpu.make_async_copy(src, dst, load_sems.at[i])
        for i, (src, dst) in enumerate((
            (x_hbm, x_ref), (in_gain_hbm, in_gain_ref), (proj_hbm, proj_ref),
            (gate_w_hbm, gate_w_ref), (out_gain_hbm, out_gain_ref), (out_w_hbm, out_w_ref),
        ))
    ]
    for load in loads:
        load.start()

    def plane_at(step):
        y_lo2 = lax.rem(y_lo + lax.rem(step // 4, 2), 2)
        pair2 = lax.rem(y_hi + step // 8, 2) * 4 + lax.rem(x + lax.rem(step, 4), 4)
        return y_lo2, pair2

    barrier = pltpu.get_barrier_semaphore()

    def greet(device):
        pl.semaphore_signal(barrier, inc=1, device_id=device, device_id_type=MESH)

    def greet_z(step, carry):
        greet((lax.rem(z + step, 8) * 2 + y_lo, col))
        return carry

    def greet_plane(step, carry):
        y_lo2, pair2 = plane_at(step)
        greet((z * 2 + y_lo2, pair2 * 2 + core))
        return carry

    lax.fori_loop(1, 8, greet_z, 0)
    lax.fori_loop(1, 16, greet_plane, 0)
    greet(sibling)

    loads[1].wait()
    loads[0].wait()
    gain = in_gain_ref[...]

    def norm_rows(values):
        values = values.astype(F32).reshape(-1, 128)
        mean = jnp.mean(values, axis=-1, keepdims=True)
        centred = values - mean
        var = jnp.mean(centred * centred, axis=-1, keepdims=True)
        return (centred * lax.rsqrt(var + EPSILON) * gain).astype(BF16)

    own_cols = pl.ds(pl.multiple_of(64 * core, 64), 64)
    away_cols = pl.ds(pl.multiple_of(64 * (1 - core), 64), 64)

    def norm_away(step, carry):
        first = pl.multiple_of(step * 4, 4)
        other[pl.ds(first, 4)] = norm_rows(x_ref[pl.ds(32 * (1 - core) + first, 4)]).reshape(4, 64, 128)
        return carry

    def norm_own(step, carry):
        first = pl.multiple_of(step * 4, 4)
        normed[pl.ds(first, 4), own_cols, :] = norm_rows(
            x_ref[pl.ds(32 * core + first, 4)]
        ).reshape(4, 64, 128)
        return carry

    lax.fori_loop(0, 8, norm_away, 0)
    lax.fori_loop(0, 8, norm_own, 0)
    for load in loads[2:]:
        load.wait()
    weights_t[...] = proj_ref[...].astype(F32).T.astype(BF16)
    gain_cols[...] = jnp.broadcast_to(out_gain_ref[...], (128, 128)).T

    pl.semaphore_wait(barrier, 23)
    swaps = []
    for part in range(4):
        swap = pltpu.make_async_remote_copy(
            src_ref=other.at[pl.ds(8 * part, 8)],
            dst_ref=normed.at[pl.ds(8 * part, 8), own_cols, :],
            send_sem=swap_sems.at[0, part], recv_sem=swap_sems.at[1, part],
            device_id=sibling, device_id_type=MESH,
        )
        swap.start()
        swaps.append(swap)

    def ready_z(step, carry):
        pl.semaphore_signal(
            ready, inc=1, device_id=(lax.rem(z + step, 8) * 2 + y_lo, col), device_id_type=MESH
        )
        return carry

    lax.fori_loop(1, 8, ready_z, 0)

    def project(first_row, part):
        half = weights_t[first_row : first_row + 256, :]

        def some(step, carry):
            first = pl.multiple_of(8 * part + step * 4, 4)
            rows = normed[pl.ds(first, 4)].reshape(512, 128)
            both = lax.dot_general(half, rows, NT, preferred_element_type=F32)
            side = sigmoid(both[128:]) * both[:128]
            for i in range(4):
                wide[pl.ds(first + i, 128, stride=32), :] = side[:, i * 128 : (i + 1) * 128]
            return carry

        lax.fori_loop(0, 2, some, 0)

    def toward(up2, dz):
        z2 = lax.rem(z + 8 + (2 * up2 - 1) * dz, 8)
        return z2, lax.rem(z2 + 7 + up2, 8)

    for part in range(4):
        swaps[part].wait()
        project(256, part)
    pl.semaphore_wait(ready, 7)
    pl.semaphore_signal(ready_core, inc=1, device_id=sibling, device_id_type=MESH)
    pl.semaphore_wait(ready_core, 1)

    def send_right(group, carry):
        dz, up2 = 3 - group // 2, lax.rem(up + group + 1, 2)
        z2, cls = toward(up2, dz)

        def narrow(step, inner):
            first = pl.multiple_of(cls * 512 + step * 128, 128)
            right_send[pl.ds(cls * 16 + step * 4, 4)] = (
                wide[pl.ds(first, 128), :].astype(BF16).reshape(4, 32, 128)
            )
            return inner

        lax.fori_loop(0, 4, narrow, 0)

        def send(step, inner):
            y_lo2, pair2 = plane_at(step)

            @pl.when(cls * 16 + y_lo2 * 8 + pair2 != me)
            def _():
                pltpu.make_async_remote_copy(
                    src_ref=right_send.at[cls * 16 + y_lo2 * 8 + pair2],
                    dst_ref=right_buf.at[row, core, pair],
                    send_sem=right_sems.at[4], recv_sem=right_sems.at[dz],
                    device_id=(z2 * 2 + y_lo2, pair2 * 2 + 1 - up2), device_id_type=MESH,
                ).start()

            return inner

        lax.fori_loop(0, 16, send, 0)
        return carry

    lax.fori_loop(0, 8, send_right, 0)
    own_right = pltpu.make_async_copy(
        right_send.at[me], right_buf.at[row, core, pair], own_sems.at[0]
    )
    own_right.start()

    for part in range(4):
        project(0, part)

    def narrow_left(step, carry):
        block = wide[pl.ds(pl.multiple_of(step * 128, 128), 128), :].astype(BF16)
        block = block.reshape(4, CHUNKS, ROWS, 128)
        for c in range(CHUNKS):
            left_send[c, pl.ds(step * 4, 4)] = block[:, c]
        return carry

    lax.fori_loop(0, 32, narrow_left, 0)

    def send_left_chunk(c):
        def send_left(step, carry):
            group = lax.rem(step, 8)
            dz, up2 = 3 - group // 2, lax.rem(up + group + 1, 2)
            z2, cls = toward(up2, dz)
            y_lo2, pair2 = plane_at(step // 8)

            @pl.when(cls * 16 + y_lo2 * 8 + pair2 != me)
            def _():
                pltpu.make_async_remote_copy(
                    src_ref=left_send.at[c, cls * 16 + y_lo2 * 8 + pair2],
                    dst_ref=left_buf.at[c, dz * 2 + y_lo, core, pair],
                    send_sem=left_sems.at[0, c], recv_sem=left_sems.at[1, c],
                    device_id=(z2 * 2 + y_lo2, pair2 * 2 + 1 - up2), device_id_type=MESH,
                ).start()

            return carry

        lax.fori_loop(0, 128, send_left, 0)
        own = pltpu.make_async_copy(
            left_send.at[c, me], left_buf.at[c, y_lo, core, pair], own_sems.at[1 + c]
        )
        own.start()
        return own

    own_left = [send_left_chunk(0)]

    def gate_rows(step, carry):
        first = pl.multiple_of(step * 4, 4)
        rows = normed[pl.ds(first, 4)].reshape(512, 128)
        gates[pl.ds(first, 4)] = sigmoid(
            jnp.dot(rows, gate_w_ref[...], preferred_element_type=F32)
        ).reshape(4, 128, 128)
        return carry

    lax.fori_loop(0, 8, gate_rows, 0)

    def wait_all(refs, count, send_sem, recv_sem):
        return pltpu.make_async_remote_copy(
            src_ref=refs.at[pl.ds(0, count)], dst_ref=refs.at[pl.ds(0, count)],
            send_sem=send_sem, recv_sem=recv_sem, device_id=sibling, device_id_type=MESH,
        )

    forwards = []
    for dz in (3, 2, 1, 0):
        if dz == 0:
            own_right.wait()
        wait_all(right_send, 32 if dz else 31, right_sems.at[4], right_sems.at[dz]).wait_recv()
        source = right_buf.at[pl.ds(2 * lax.rem(z + 8 + (1 - 2 * up) * dz, 8), 2)]
        forward = pltpu.make_async_remote_copy(
            src_ref=source, dst_ref=source,
            send_sem=fwd_sems.at[0, dz], recv_sem=fwd_sems.at[1, dz],
            device_id=partner, device_id_type=MESH,
        )
        forward.start()
        forwards.append(forward)
    for c in range(1, CHUNKS):
        own_left.append(send_left_chunk(c))
    for forward in forwards:
        forward.wait()

    for c in range(CHUNKS):
        own_left[c].wait()
        wait_all(left_send.at[c], 127, left_sems.at[0, c], left_sems.at[1, c]).wait_recv()

        def columns(step, carry, c=c):
            n = lax.rem(step + pair // 2, 4)
            total = None
            for k in range(4):
                left = jnp.concatenate(
                    [left_buf[c, :, :, 2 * k + s].reshape(16 * ROWS, 128) for s in range(2)], axis=-1
                )
                right = jnp.concatenate(
                    [right_buf[pl.ds(4 * n, 4), :, 2 * k + s].reshape(256, 128) for s in range(2)],
                    axis=-1,
                )
                term = lax.dot_general(left, right, NT, preferred_element_type=F32)
                total = term if total is None else total + term
            tiles = total.astype(BF16).reshape(8, 2, ROWS, 256)
            for s in range(2):
                tri_send[c, :, :, 2 * n + s] = tiles[..., s * 128 : (s + 1) * 128]

            def send_tri(part, inner):
                dz, rest = 3 - lax.rem(part, 4), part // 4
                core2, y_lo2 = lax.rem(rest, 2), lax.rem(y_lo + lax.rem(rest // 2, 2), 2)
                pair2 = 2 * n + lax.rem(pair + rest // 4, 2)
                row2 = lax.rem(z + 8 + (1 - 2 * up) * dz, 8) * 2 + y_lo2
                col2 = pair2 * 2 + core2

                @pl.when(row2 * 16 + col2 != row * 16 + col)
                def _():
                    pltpu.make_async_remote_copy(
                        src_ref=tri_send.at[c, dz * 2 + y_lo2, core2, pair2],
                        dst_ref=tri_buf.at[c, me],
                        send_sem=tri_sems.at[0, c], recv_sem=tri_sems.at[1, c],
                        device_id=(row2, col2), device_id_type=MESH,
                    ).start()

                return inner

            lax.fori_loop(0, 32, send_tri, 0)
            return carry

        lax.fori_loop(0, 4, columns, 0)
        own = pltpu.make_async_copy(
            tri_send.at[c, y_lo, core, pair], tri_buf.at[c, me], own_sems.at[1 + CHUNKS + c]
        )
        own.start()
        own.wait()

    outs = []
    for c in range(CHUNKS):
        wait_all(left_send.at[c], 127, tri_sems.at[0, c], tri_sems.at[1, c]).wait_recv()

        def add(h, acc, c=c):
            return acc + tri_buf[c, h].astype(F32)

        mean = lax.fori_loop(0, 128, add, jnp.zeros((ROWS, 128), F32), unroll=8) * (1.0 / 128.0)

        def add_square(h, acc, c=c, mean=mean):
            centred = tri_buf[c, h].astype(F32) - mean
            wide[pl.ds(pl.multiple_of(h * ROWS, ROWS), ROWS), :] = centred
            return acc + centred * centred

        var = lax.fori_loop(0, 128, add_square, jnp.zeros((ROWS, 128), F32), unroll=8) * (1.0 / 128.0)
        scale = lax.rsqrt(var + EPSILON)
        scales = gain_cols[...]
        for i in range(ROWS):
            tile = wide[pl.ds(i, 128, stride=ROWS), :] * scale[i : i + 1, :] * scales
            projected = lax.dot_general(
                tile.astype(BF16), out_w_ref[...], TN, preferred_element_type=F32
            )
            result[c * ROWS + i] = (gates[c * ROWS + i] * projected).astype(BF16)

        rows = pl.ds(c * ROWS, ROWS)
        place_rows = pl.ds(32 * core + c * ROWS, ROWS)
        keep = pltpu.make_async_copy(
            result.at[rows, own_cols, :], o_ref.at[place_rows], out_sems.at[2, c]
        )
        keep.start()
        give = pltpu.make_async_remote_copy(
            src_ref=result.at[rows, away_cols, :], dst_ref=o_ref.at[place_rows],
            send_sem=out_sems.at[0, c], recv_sem=out_sems.at[1, c],
            device_id=sibling, device_id_type=MESH,
        )
        give.start()
        outs += [keep, give]
    wait_all(right_send, 127, right_sems.at[4], right_sems.at[0]).wait_send()
    for c in range(CHUNKS):
        wait_all(left_send.at[c], 127, left_sems.at[0, c], left_sems.at[1, c]).wait_send()
        wait_all(left_send.at[c], 127, tri_sems.at[0, c], tri_sems.at[1, c]).wait_send()
    for out in outs:
        out.wait()


def shards(pair_rep, in_gain, proj_weight, gate_weight, out_gain, out_weight):
    anywhere = pl.BlockSpec(memory_space=pl.ANY)
    return pl.pallas_call(
        kernel,
        out_shape=jax.ShapeDtypeStruct((64, 64, 128), BF16),
        in_specs=[anywhere] * 6,
        out_specs=anywhere,
        scratch_shapes=[
            pltpu.VMEM((64, 64, 128), BF16),
            pltpu.VMEM((1, 128), F32),
            pltpu.VMEM((128, 512), BF16),
            pltpu.VMEM((128, 128), BF16),
            pltpu.VMEM((1, 128), F32),
            pltpu.VMEM((128, 128), BF16),
            pltpu.VMEM((32, 128, 128), BF16),
            pltpu.VMEM((32, 64, 128), BF16),
            pltpu.VMEM((128 * 32, 128), F32),
            pltpu.VMEM((128, 32, 128), BF16),
            pltpu.VMEM((CHUNKS, 128, ROWS, 128), BF16),
            pltpu.VMEM((16, 2, 8, 32, 128), BF16),
            pltpu.VMEM((CHUNKS, 8, 2, 8, ROWS, 128), BF16),
            pltpu.VMEM((CHUNKS, 8, 2, 8, ROWS, 128), BF16),
            pltpu.VMEM((CHUNKS, 128, ROWS, 128), BF16),
            pltpu.VMEM((32, 128, 128), F32),
            pltpu.VMEM((32, 128, 128), BF16),
            pltpu.VMEM((512, 128), BF16),
            pltpu.VMEM((128, 128), F32),
            pltpu.SemaphoreType.REGULAR,
            pltpu.SemaphoreType.REGULAR,
            pltpu.SemaphoreType.DMA((6,)),
            pltpu.SemaphoreType.DMA((2, 4)),
            pltpu.SemaphoreType.DMA((5,)),
            pltpu.SemaphoreType.DMA((1 + 2 * CHUNKS,)),
            pltpu.SemaphoreType.DMA((2, 4)),
            pltpu.SemaphoreType.DMA((2, CHUNKS)),
            pltpu.SemaphoreType.DMA((2, CHUNKS)),
            pltpu.SemaphoreType.DMA((3, CHUNKS)),
        ],
        compiler_params=pltpu.CompilerParams(
            collective_id=0, has_side_effects=True, vmem_limit_bytes=60 * 2**20
        ),
    )(
        pair_rep, in_gain.reshape(1, 128), proj_weight, gate_weight,
        out_gain.reshape(1, 128), out_weight,
    )


def solution(mesh):
    return jax.shard_map(
        shards,
        mesh=mesh,
        in_specs=(P("row", "col", None), P(), P(), P(), P(), P()),
        out_specs=P("row", "col", None),
        check_vma=False,
    )
```

```python
import jax
import jax.numpy as jnp
from jax import lax
from jax.experimental import pallas as pl
from jax.experimental.pallas import tpu as pltpu
from jax.sharding import PartitionSpec as P

EPSILON = 1e-05
MESH = pl.DeviceIdType.MESH
F32, BF16 = jnp.float32, jnp.bfloat16

CHUNKS = 2
ROWS = 32 // CHUNKS
NT = (((1,), (1,)), ((), ()))
TN = (((0,), (0,)), ((), ()))


def sigmoid(values):
    return 0.5 * jnp.tanh(0.5 * values) + 0.5


def kernel(
    x_hbm, in_gain_hbm, proj_hbm, gate_w_hbm, out_gain_hbm, out_w_hbm, o_ref,
    x_ref, in_gain_ref, proj_ref, gate_w_ref, out_gain_ref, out_w_ref,
    normed, other, wide, right_send, left_send, right_buf, left_buf,
    tri_send, tri_buf, gates, result, weights_t, gain_cols,
    ready, load_sems, swap_sems, right_sems, own_sems, fwd_sems,
    left_sems, tri_sems, out_sems,
):
    row, col = lax.axis_index("row"), lax.axis_index("col")
    z, y_lo = row // 2, lax.rem(row, 2)
    pair, core = col // 2, lax.rem(col, 2)
    y_hi, x = pair // 4, lax.rem(pair, 4)
    place = y_lo * 8 + pair
    up = 1 - core
    me = lax.rem(z + 8 - core, 8) * 16 + place
    sibling = (row, pair * 2 + 1 - core)
    partner = (lax.rem(z + 7 + 2 * up, 8) * 2 + y_lo, pair * 2 + 1 - core)

    loads = [
        pltpu.make_async_copy(src, dst, load_sems.at[i])
        for i, (src, dst) in enumerate((
            (x_hbm, x_ref), (in_gain_hbm, in_gain_ref), (proj_hbm, proj_ref),
            (gate_w_hbm, gate_w_ref), (out_gain_hbm, out_gain_ref), (out_w_hbm, out_w_ref),
        ))
    ]
    for load in loads:
        load.start()

    def plane_at(step):
        y_lo2 = lax.rem(y_lo + lax.rem(step // 4, 2), 2)
        pair2 = lax.rem(y_hi + step // 8, 2) * 4 + lax.rem(x + lax.rem(step, 4), 4)
        return y_lo2, pair2

    barrier = pltpu.get_barrier_semaphore()

    def greet(device):
        pl.semaphore_signal(barrier, inc=1, device_id=device, device_id_type=MESH)

    def near_z(step):
        return lax.rem(z + step + step // 4, 8) * 2 + y_lo

    def greet_z(step, carry):
        greet((near_z(step), col))
        return carry

    def greet_plane(step, carry):
        y_lo2, pair2 = plane_at(step)
        for core2 in range(2):
            greet((z * 2 + y_lo2, pair2 * 2 + core2))
        return carry

    lax.fori_loop(1, 7, greet_z, 0)
    lax.fori_loop(1, 16, greet_plane, 0)
    greet(sibling)

    loads[1].wait()
    loads[0].wait()
    gain = in_gain_ref[...]

    def norm_rows(values):
        values = values.astype(F32).reshape(-1, 128)
        mean = jnp.mean(values, axis=-1, keepdims=True)
        centred = values - mean
        var = jnp.mean(centred * centred, axis=-1, keepdims=True)
        return (centred * lax.rsqrt(var + EPSILON) * gain).astype(BF16)

    own_cols = pl.ds(pl.multiple_of(64 * core, 64), 64)
    away_cols = pl.ds(pl.multiple_of(64 * (1 - core), 64), 64)

    def norm_away(step, carry):
        first = pl.multiple_of(step * 4, 4)
        other[pl.ds(first, 4)] = norm_rows(x_ref[pl.ds(32 * (1 - core) + first, 4)]).reshape(4, 64, 128)
        return carry

    def norm_own(step, carry):
        first = pl.multiple_of(step * 4, 4)
        normed[pl.ds(first, 4), own_cols, :] = norm_rows(
            x_ref[pl.ds(32 * core + first, 4)]
        ).reshape(4, 64, 128)
        return carry

    lax.fori_loop(0, 8, norm_away, 0)
    for load in loads[2:]:
        load.wait()
    weights_t[...] = proj_ref[...].astype(F32).T.astype(BF16)

    pl.semaphore_wait(barrier, 37)

    def ready_z(step, carry):
        pl.semaphore_signal(
            ready, inc=1, device_id=(near_z(step), col), device_id_type=MESH
        )
        return carry

    lax.fori_loop(1, 7, ready_z, 0)
    swaps = []
    for part in range(4):
        swap = pltpu.make_async_remote_copy(
            src_ref=other.at[pl.ds(8 * part, 8)],
            dst_ref=normed.at[pl.ds(8 * part, 8), own_cols, :],
            send_sem=swap_sems.at[0, part], recv_sem=swap_sems.at[1, part],
            device_id=sibling, device_id_type=MESH,
        )
        swap.start()
        swaps.append(swap)

    lax.fori_loop(0, 8, norm_own, 0)

    def project(first_row, part):
        half = weights_t[first_row : first_row + 256, :]

        def some(step, carry):
            first = pl.multiple_of(8 * part + step * 4, 4)
            rows = normed[pl.ds(first, 4)].reshape(512, 128)
            both = lax.dot_general(half, rows, NT, preferred_element_type=F32)
            side = sigmoid(both[128:]) * both[:128]
            for i in range(4):
                wide[pl.ds(first + i, 128, stride=32), :] = side[:, i * 128 : (i + 1) * 128]
            return carry

        lax.fori_loop(0, 2, some, 0)

    def toward(up2, dz):
        z2 = lax.rem(z + 8 + (2 * up2 - 1) * dz, 8)
        return z2, lax.rem(z2 + 7 + up2, 8)

    for part in range(4):
        swaps[part].wait()
        project(256, part)
    pl.semaphore_wait(ready, 6)

    def send_right(group, carry):
        dz, up2 = 3 - group // 2, lax.rem(up + group + 1, 2)
        z2, cls = toward(up2, dz)

        def narrow(step, inner):
            first = pl.multiple_of(cls * 512 + step * 128, 128)
            right_send[pl.ds(cls * 16 + step * 4, 4)] = (
                wide[pl.ds(first, 128), :].astype(BF16).reshape(4, 32, 128)
            )
            return inner

        lax.fori_loop(0, 4, narrow, 0)

        def send(step, inner):
            y_lo2, pair2 = plane_at(step)

            @pl.when(cls * 16 + y_lo2 * 8 + pair2 != me)
            def _():
                pltpu.make_async_remote_copy(
                    src_ref=right_send.at[cls * 16 + y_lo2 * 8 + pair2],
                    dst_ref=right_buf.at[row, core, pair],
                    send_sem=right_sems.at[4], recv_sem=right_sems.at[dz],
                    device_id=(z2 * 2 + y_lo2, pair2 * 2 + 1 - up2), device_id_type=MESH,
                ).start()

            return inner

        lax.fori_loop(0, 16, send, 0)
        return carry

    lax.fori_loop(0, 8, send_right, 0)
    own_right = pltpu.make_async_copy(
        right_send.at[me], right_buf.at[row, core, pair], own_sems.at[0]
    )
    own_right.start()

    for part in range(4):
        project(0, part)

    def narrow_left(step, carry):
        block = wide[pl.ds(pl.multiple_of(step * 128, 128), 128), :].astype(BF16)
        block = block.reshape(4, CHUNKS, ROWS, 128)
        for c in range(CHUNKS):
            left_send[c, pl.ds(step * 4, 4)] = block[:, c]
        return carry

    lax.fori_loop(0, 32, narrow_left, 0)

    def send_left_chunk(c):
        def send_left(step, carry):
            group = lax.rem(step, 8)
            dz, up2 = 3 - group // 2, lax.rem(up + group + 1, 2)
            z2, cls = toward(up2, dz)
            y_lo2, pair2 = plane_at(step // 8)

            @pl.when(cls * 16 + y_lo2 * 8 + pair2 != me)
            def _():
                pltpu.make_async_remote_copy(
                    src_ref=left_send.at[c, cls * 16 + y_lo2 * 8 + pair2],
                    dst_ref=left_buf.at[c, dz * 2 + y_lo, core, pair],
                    send_sem=left_sems.at[0, c], recv_sem=left_sems.at[1, c],
                    device_id=(z2 * 2 + y_lo2, pair2 * 2 + 1 - up2), device_id_type=MESH,
                ).start()

            return carry

        lax.fori_loop(0, 128, send_left, 0)
        own = pltpu.make_async_copy(
            left_send.at[c, me], left_buf.at[c, y_lo, core, pair], own_sems.at[1 + c]
        )
        own.start()
        return own

    own_left = [send_left_chunk(0)]

    gain_cols[...] = jnp.broadcast_to(out_gain_ref[...], (128, 128)).T
    def gate_rows(step, carry):
        first = pl.multiple_of(step * 4, 4)
        rows = normed[pl.ds(first, 4)].reshape(512, 128)
        gates[pl.ds(first, 4)] = sigmoid(
            jnp.dot(rows, gate_w_ref[...], preferred_element_type=F32)
        ).reshape(4, 128, 128)
        return carry

    lax.fori_loop(0, 8, gate_rows, 0)

    def wait_all(refs, count, send_sem, recv_sem):
        return pltpu.make_async_remote_copy(
            src_ref=refs.at[pl.ds(0, count)], dst_ref=refs.at[pl.ds(0, count)],
            send_sem=send_sem, recv_sem=recv_sem, device_id=sibling, device_id_type=MESH,
        )

    forwards = []
    for dz in (3, 2, 1, 0):
        if dz == 0:
            own_right.wait()
        wait_all(right_send, 32 if dz else 31, right_sems.at[4], right_sems.at[dz]).wait_recv()
        source = right_buf.at[pl.ds(2 * lax.rem(z + 8 + (1 - 2 * up) * dz, 8), 2)]
        forward = pltpu.make_async_remote_copy(
            src_ref=source, dst_ref=source,
            send_sem=fwd_sems.at[0, dz], recv_sem=fwd_sems.at[1, dz],
            device_id=partner, device_id_type=MESH,
        )
        forward.start()
        forwards.append(forward)
    for c in range(1, CHUNKS):
        own_left.append(send_left_chunk(c))
    for forward in forwards:
        forward.wait()

    for c in range(CHUNKS):
        own_left[c].wait()
        wait_all(left_send.at[c], 127, left_sems.at[0, c], left_sems.at[1, c]).wait_recv()

        def columns(step, carry, c=c):
            n = lax.rem(step + pair // 2, 4)
            total = None
            for k in range(4):
                left = jnp.concatenate(
                    [left_buf[c, :, :, 2 * k + s].reshape(16 * ROWS, 128) for s in range(2)], axis=-1
                )
                right = jnp.concatenate(
                    [right_buf[pl.ds(4 * n, 4), :, 2 * k + s].reshape(256, 128) for s in range(2)],
                    axis=-1,
                )
                term = lax.dot_general(left, right, NT, preferred_element_type=F32)
                total = term if total is None else total + term
            tiles = total.astype(BF16).reshape(8, 2, ROWS, 256)
            for s in range(2):
                tri_send[c, :, :, 2 * n + s] = tiles[..., s * 128 : (s + 1) * 128]

            def send_tri(part, inner):
                dz, rest = 3 - lax.rem(part, 4), part // 4
                core2, y_lo2 = lax.rem(rest, 2), lax.rem(y_lo + lax.rem(rest // 2, 2), 2)
                pair2 = 2 * n + lax.rem(pair + rest // 4, 2)
                row2 = lax.rem(z + 8 + (1 - 2 * up) * dz, 8) * 2 + y_lo2
                col2 = pair2 * 2 + core2

                @pl.when(row2 * 16 + col2 != row * 16 + col)
                def _():
                    pltpu.make_async_remote_copy(
                        src_ref=tri_send.at[c, dz * 2 + y_lo2, core2, pair2],
                        dst_ref=tri_buf.at[c, me],
                        send_sem=tri_sems.at[0, c], recv_sem=tri_sems.at[1, c],
                        device_id=(row2, col2), device_id_type=MESH,
                    ).start()

                return inner

            lax.fori_loop(0, 32, send_tri, 0)
            return carry

        lax.fori_loop(0, 4, columns, 0)
        own = pltpu.make_async_copy(
            tri_send.at[c, y_lo, core, pair], tri_buf.at[c, me], own_sems.at[1 + CHUNKS + c]
        )
        own.start()
        own.wait()

    outs = []
    for c in range(CHUNKS):
        wait_all(left_send.at[c], 127, tri_sems.at[0, c], tri_sems.at[1, c]).wait_recv()

        def add(h, acc, c=c):
            return acc + tri_buf[c, h].astype(F32)

        mean = lax.fori_loop(0, 128, add, jnp.zeros((ROWS, 128), F32), unroll=8) * (1.0 / 128.0)

        def add_square(h, acc, c=c, mean=mean):
            centred = tri_buf[c, h].astype(F32) - mean
            wide[pl.ds(pl.multiple_of(h * ROWS, ROWS), ROWS), :] = centred
            return acc + centred * centred

        var = lax.fori_loop(0, 128, add_square, jnp.zeros((ROWS, 128), F32), unroll=8) * (1.0 / 128.0)
        scale = lax.rsqrt(var + EPSILON)
        scales = gain_cols[...]
        for i in range(ROWS):
            tile = wide[pl.ds(i, 128, stride=ROWS), :] * scale[i : i + 1, :] * scales
            projected = lax.dot_general(
                tile.astype(BF16), out_w_ref[...], TN, preferred_element_type=F32
            )
            result[c * ROWS + i] = (gates[c * ROWS + i] * projected).astype(BF16)

        rows = pl.ds(c * ROWS, ROWS)
        place_rows = pl.ds(32 * core + c * ROWS, ROWS)
        keep = pltpu.make_async_copy(
            result.at[rows, own_cols, :], o_ref.at[place_rows], out_sems.at[2, c]
        )
        keep.start()
        give = pltpu.make_async_remote_copy(
            src_ref=result.at[rows, away_cols, :], dst_ref=o_ref.at[place_rows],
            send_sem=out_sems.at[0, c], recv_sem=out_sems.at[1, c],
            device_id=sibling, device_id_type=MESH,
        )
        give.start()
        outs += [keep, give]
    wait_all(right_send, 127, right_sems.at[4], right_sems.at[0]).wait_send()
    for c in range(CHUNKS):
        wait_all(left_send.at[c], 127, left_sems.at[0, c], left_sems.at[1, c]).wait_send()
        wait_all(left_send.at[c], 127, tri_sems.at[0, c], tri_sems.at[1, c]).wait_send()
    for out in outs:
        out.wait()


def shards(pair_rep, in_gain, proj_weight, gate_weight, out_gain, out_weight):
    anywhere = pl.BlockSpec(memory_space=pl.ANY)
    return pl.pallas_call(
        kernel,
        out_shape=jax.ShapeDtypeStruct((64, 64, 128), BF16),
        in_specs=[anywhere] * 6,
        out_specs=anywhere,
        scratch_shapes=[
            pltpu.VMEM((64, 64, 128), BF16),
            pltpu.VMEM((1, 128), F32),
            pltpu.VMEM((128, 512), BF16),
            pltpu.VMEM((128, 128), BF16),
            pltpu.VMEM((1, 128), F32),
            pltpu.VMEM((128, 128), BF16),
            pltpu.VMEM((32, 128, 128), BF16),
            pltpu.VMEM((32, 64, 128), BF16),
            pltpu.VMEM((128 * 32, 128), F32),
            pltpu.VMEM((128, 32, 128), BF16),
            pltpu.VMEM((CHUNKS, 128, ROWS, 128), BF16),
            pltpu.VMEM((16, 2, 8, 32, 128), BF16),
            pltpu.VMEM((CHUNKS, 8, 2, 8, ROWS, 128), BF16),
            pltpu.VMEM((CHUNKS, 8, 2, 8, ROWS, 128), BF16),
            pltpu.VMEM((CHUNKS, 128, ROWS, 128), BF16),
            pltpu.VMEM((32, 128, 128), F32),
            pltpu.VMEM((32, 128, 128), BF16),
            pltpu.VMEM((512, 128), BF16),
            pltpu.VMEM((128, 128), F32),
            pltpu.SemaphoreType.REGULAR,
            pltpu.SemaphoreType.DMA((6,)),
            pltpu.SemaphoreType.DMA((2, 4)),
            pltpu.SemaphoreType.DMA((5,)),
            pltpu.SemaphoreType.DMA((1 + 2 * CHUNKS,)),
            pltpu.SemaphoreType.DMA((2, 4)),
            pltpu.SemaphoreType.DMA((2, CHUNKS)),
            pltpu.SemaphoreType.DMA((2, CHUNKS)),
            pltpu.SemaphoreType.DMA((3, CHUNKS)),
        ],
        compiler_params=pltpu.CompilerParams(
            collective_id=0, has_side_effects=True, vmem_limit_bytes=60 * 2**20
        ),
    )(
        pair_rep, in_gain.reshape(1, 128), proj_weight, gate_weight,
        out_gain.reshape(1, 128), out_weight,
    )


def solution(mesh):
    return jax.shard_map(
        shards,
        mesh=mesh,
        in_specs=(P("row", "col", None), P(), P(), P(), P(), P()),
        out_specs=P("row", "col", None),
        check_vma=False,
    )
```

```python
import jax
import jax.numpy as jnp
from jax import lax
from jax.experimental import pallas as pl
from jax.experimental.pallas import tpu as pltpu
from jax.sharding import PartitionSpec as P

EPSILON = 1e-05
MESH = pl.DeviceIdType.MESH
F32, BF16 = jnp.float32, jnp.bfloat16

CHUNKS = 2
ROWS = 32 // CHUNKS
NT = (((1,), (1,)), ((), ()))
TN = (((0,), (0,)), ((), ()))


def sigmoid(values):
    return 0.5 * jnp.tanh(0.5 * values) + 0.5


def kernel(
    x_hbm, in_gain_hbm, proj_hbm, gate_w_hbm, out_gain_hbm, out_w_hbm, o_ref,
    x_ref, in_gain_ref, proj_ref, gate_w_ref, out_gain_ref, out_w_ref,
    normed, other, wide, right_send, left_send, right_buf, left_buf,
    tri_send, tri_buf, gates, result, weights_t, gain_cols,
    ready, load_sems, swap_sems, right_sems, own_sems, fwd_sems,
    left_sems, tri_sems, out_sems,
):
    row, col = lax.axis_index("row"), lax.axis_index("col")
    z, y_lo = row // 2, lax.rem(row, 2)
    pair, core = col // 2, lax.rem(col, 2)
    y_hi, x = pair // 4, lax.rem(pair, 4)
    place = y_lo * 8 + pair
    up = 1 - core
    me = lax.rem(z + 8 - core, 8) * 16 + place
    sibling = (row, pair * 2 + 1 - core)
    partner = (lax.rem(z + 7 + 2 * up, 8) * 2 + y_lo, pair * 2 + 1 - core)

    loads = [
        pltpu.make_async_copy(src, dst, load_sems.at[i])
        for i, (src, dst) in enumerate((
            (x_hbm, x_ref), (in_gain_hbm, in_gain_ref), (proj_hbm, proj_ref),
            (gate_w_hbm, gate_w_ref), (out_gain_hbm, out_gain_ref), (out_w_hbm, out_w_ref),
        ))
    ]
    for load in loads:
        load.start()

    def plane_at(step):
        y_lo2 = lax.rem(y_lo + lax.rem(step // 4, 2), 2)
        pair2 = lax.rem(y_hi + step // 8, 2) * 4 + lax.rem(x + lax.rem(step, 4), 4)
        return y_lo2, pair2

    barrier = pltpu.get_barrier_semaphore()

    def greet(device):
        pl.semaphore_signal(barrier, inc=1, device_id=device, device_id_type=MESH)

    def near_z(step):
        return lax.rem(z + step + step // 4, 8) * 2 + y_lo

    def greet_z(step, carry):
        greet((near_z(step), col))
        return carry

    def greet_plane(step, carry):
        y_lo2, pair2 = plane_at(step)
        for core2 in range(2):
            greet((z * 2 + y_lo2, pair2 * 2 + core2))
        return carry

    lax.fori_loop(1, 7, greet_z, 0)
    lax.fori_loop(1, 16, greet_plane, 0)
    greet(sibling)

    loads[1].wait()
    loads[0].wait()
    gain = in_gain_ref[...]

    def norm_rows(values):
        values = values.astype(F32).reshape(-1, 128)
        mean = jnp.mean(values, axis=-1, keepdims=True)
        centred = values - mean
        var = jnp.mean(centred * centred, axis=-1, keepdims=True)
        return (centred * lax.rsqrt(var + EPSILON) * gain).astype(BF16)

    own_cols = pl.ds(pl.multiple_of(64 * core, 64), 64)
    away_cols = pl.ds(pl.multiple_of(64 * (1 - core), 64), 64)

    def norm_away(step, carry):
        first = pl.multiple_of(step * 4, 4)
        other[pl.ds(first, 4)] = norm_rows(x_ref[pl.ds(32 * (1 - core) + first, 4)]).reshape(4, 64, 128)
        return carry

    def norm_own(step, carry):
        first = pl.multiple_of(step * 4, 4)
        normed[pl.ds(first, 4), own_cols, :] = norm_rows(
            x_ref[pl.ds(32 * core + first, 4)]
        ).reshape(4, 64, 128)
        return carry

    lax.fori_loop(0, 8, norm_away, 0)
    for load in loads[2:]:
        load.wait()
    weights_t[...] = proj_ref[...].astype(F32).T.astype(BF16)

    pl.semaphore_wait(barrier, 37)

    def ready_z(step, carry):
        pl.semaphore_signal(
            ready, inc=1, device_id=(near_z(step), col), device_id_type=MESH
        )
        return carry

    lax.fori_loop(1, 7, ready_z, 0)
    swaps = []
    for part in range(4):
        swap = pltpu.make_async_remote_copy(
            src_ref=other.at[pl.ds(8 * part, 8)],
            dst_ref=normed.at[pl.ds(8 * part, 8), own_cols, :],
            send_sem=swap_sems.at[0, part], recv_sem=swap_sems.at[1, part],
            device_id=sibling, device_id_type=MESH,
        )
        swap.start()
        swaps.append(swap)

    lax.fori_loop(0, 8, norm_own, 0)

    def project(first_row, part):
        half = weights_t[first_row : first_row + 256, :]

        def some(step, carry):
            first = pl.multiple_of(8 * part + step * 4, 4)
            rows = normed[pl.ds(first, 4)].reshape(512, 128)
            both = lax.dot_general(half, rows, NT, preferred_element_type=F32)
            side = sigmoid(both[128:]) * both[:128]
            for i in range(4):
                wide[pl.ds(first + i, 128, stride=32), :] = side[:, i * 128 : (i + 1) * 128]
            return carry

        lax.fori_loop(0, 2, some, 0)

    def toward(up2, dz):
        z2 = lax.rem(z + 8 + (2 * up2 - 1) * dz, 8)
        return z2, lax.rem(z2 + 7 + up2, 8)

    for part in range(4):
        swaps[part].wait()
        project(256, part)
    pl.semaphore_wait(ready, 6)

    def send_right(group, carry):
        dz, up2 = 3 - group // 2, lax.rem(up + group + 1, 2)
        z2, cls = toward(up2, dz)

        def narrow(step, inner):
            first = pl.multiple_of(cls * 512 + step * 128, 128)
            right_send[pl.ds(cls * 16 + step * 4, 4)] = (
                wide[pl.ds(first, 128), :].astype(BF16).reshape(4, 32, 128)
            )
            return inner

        lax.fori_loop(0, 4, narrow, 0)

        def send(step, inner):
            y_lo2, pair2 = plane_at(step)

            @pl.when(cls * 16 + y_lo2 * 8 + pair2 != me)
            def _():
                pltpu.make_async_remote_copy(
                    src_ref=right_send.at[cls * 16 + y_lo2 * 8 + pair2],
                    dst_ref=right_buf.at[row, core, pair],
                    send_sem=right_sems.at[4], recv_sem=right_sems.at[dz],
                    device_id=(z2 * 2 + y_lo2, pair2 * 2 + 1 - up2), device_id_type=MESH,
                ).start()

            return inner

        lax.fori_loop(0, 16, send, 0)
        return carry

    lax.fori_loop(0, 8, send_right, 0)
    own_right = pltpu.make_async_copy(
        right_send.at[me], right_buf.at[row, core, pair], own_sems.at[0]
    )
    own_right.start()

    for part in range(4):
        project(0, part)

    def narrow_left(step, carry):
        block = wide[pl.ds(pl.multiple_of(step * 128, 128), 128), :].astype(BF16)
        block = block.reshape(4, CHUNKS, ROWS, 128)
        for c in range(CHUNKS):
            left_send[c, pl.ds(step * 4, 4)] = block[:, c]
        return carry

    lax.fori_loop(0, 32, narrow_left, 0)

    def send_left_chunk(c):
        def send_left(step, carry):
            group = lax.rem(step, 8)
            dz, up2 = 3 - group // 2, lax.rem(up + group + 1, 2)
            z2, cls = toward(up2, dz)
            y_lo2, pair2 = plane_at(step // 8)

            @pl.when(cls * 16 + y_lo2 * 8 + pair2 != me)
            def _():
                pltpu.make_async_remote_copy(
                    src_ref=left_send.at[c, cls * 16 + y_lo2 * 8 + pair2],
                    dst_ref=left_buf.at[c, dz * 2 + y_lo, core, pair],
                    send_sem=left_sems.at[0, c], recv_sem=left_sems.at[1, c],
                    device_id=(z2 * 2 + y_lo2, pair2 * 2 + 1 - up2), device_id_type=MESH,
                ).start()

            return carry

        lax.fori_loop(0, 128, send_left, 0)
        own = pltpu.make_async_copy(
            left_send.at[c, me], left_buf.at[c, y_lo, core, pair], own_sems.at[1 + c]
        )
        own.start()
        return own

    own_left = [send_left_chunk(0)]

    gain_cols[...] = jnp.broadcast_to(out_gain_ref[...], (128, 128)).T
    def gate_rows(step, carry):
        first = pl.multiple_of(step * 4, 4)
        rows = normed[pl.ds(first, 4)].reshape(512, 128)
        gates[pl.ds(first, 4)] = sigmoid(
            jnp.dot(rows, gate_w_ref[...], preferred_element_type=F32)
        ).reshape(4, 128, 128)
        return carry

    lax.fori_loop(0, 8, gate_rows, 0)

    def wait_all(refs, count, send_sem, recv_sem):
        return pltpu.make_async_remote_copy(
            src_ref=refs.at[pl.ds(0, count)], dst_ref=refs.at[pl.ds(0, count)],
            send_sem=send_sem, recv_sem=recv_sem, device_id=sibling, device_id_type=MESH,
        )

    forwards = []
    for dz in (3, 2, 1, 0):
        if dz == 0:
            own_right.wait()
        wait_all(right_send, 32 if dz else 31, right_sems.at[4], right_sems.at[dz]).wait_recv()
        source = right_buf.at[pl.ds(2 * lax.rem(z + 8 + (1 - 2 * up) * dz, 8), 2)]
        forward = pltpu.make_async_remote_copy(
            src_ref=source, dst_ref=source,
            send_sem=fwd_sems.at[0, dz], recv_sem=fwd_sems.at[1, dz],
            device_id=partner, device_id_type=MESH,
        )
        forward.start()
        forwards.append(forward)
    for c in range(1, CHUNKS):
        own_left.append(send_left_chunk(c))
    for forward in forwards:
        forward.wait()

    for c in range(CHUNKS):
        own_left[c].wait()
        wait_all(left_send.at[c], 127, left_sems.at[0, c], left_sems.at[1, c]).wait_recv()

        def columns(step, carry, c=c):
            n = lax.rem(step + pair // 2, 4)
            total = None
            for k in range(4):
                left = jnp.concatenate(
                    [left_buf[c, :, :, 2 * k + s].reshape(16 * ROWS, 128) for s in range(2)], axis=-1
                )
                right = jnp.concatenate(
                    [right_buf[pl.ds(4 * n, 4), :, 2 * k + s].reshape(256, 128) for s in range(2)],
                    axis=-1,
                )
                term = lax.dot_general(left, right, NT, preferred_element_type=F32)
                total = term if total is None else total + term
            tiles = total.astype(BF16).reshape(8, 2, ROWS, 256)
            for s in range(2):
                tri_send[c, :, :, 2 * n + s] = tiles[..., s * 128 : (s + 1) * 128]

            def send_tri(part, inner):
                dz, rest = 3 - lax.rem(part, 4), part // 4
                core2, y_lo2 = lax.rem(rest, 2), lax.rem(y_lo + lax.rem(rest // 2, 2), 2)
                pair2 = 2 * n + lax.rem(pair + rest // 4, 2)
                row2 = lax.rem(z + 8 + (1 - 2 * up) * dz, 8) * 2 + y_lo2
                col2 = pair2 * 2 + core2

                @pl.when(row2 * 16 + col2 != row * 16 + col)
                def _():
                    pltpu.make_async_remote_copy(
                        src_ref=tri_send.at[c, dz * 2 + y_lo2, core2, pair2],
                        dst_ref=tri_buf.at[c, me],
                        send_sem=tri_sems.at[0, c], recv_sem=tri_sems.at[1, c],
                        device_id=(row2, col2), device_id_type=MESH,
                    ).start()

                return inner

            lax.fori_loop(0, 32, send_tri, 0)
            return carry

        lax.fori_loop(0, 4, columns, 0)
        own = pltpu.make_async_copy(
            tri_send.at[c, y_lo, core, pair], tri_buf.at[c, me], own_sems.at[1 + CHUNKS + c]
        )
        own.start()
        own.wait()

    outs = []
    for c in range(CHUNKS):
        wait_all(left_send.at[c], 127, tri_sems.at[0, c], tri_sems.at[1, c]).wait_recv()

        def add(h, acc, c=c):
            return acc + tri_buf[c, h].astype(F32)

        mean = lax.fori_loop(0, 128, add, jnp.zeros((ROWS, 128), F32), unroll=8) * (1.0 / 128.0)

        def add_square(h, acc, c=c, mean=mean):
            centred = tri_buf[c, h].astype(F32) - mean
            wide[pl.ds(pl.multiple_of(h * ROWS, ROWS), ROWS), :] = centred
            return acc + centred * centred

        var = lax.fori_loop(0, 128, add_square, jnp.zeros((ROWS, 128), F32), unroll=8) * (1.0 / 128.0)
        scale = lax.rsqrt(var + EPSILON)
        scales = gain_cols[...]
        for i in range(ROWS):
            tile = wide[pl.ds(i, 128, stride=ROWS), :] * scale[i : i + 1, :] * scales
            projected = lax.dot_general(
                tile.astype(BF16), out_w_ref[...], TN, preferred_element_type=F32
            )
            result[c * ROWS + i] = (gates[c * ROWS + i] * projected).astype(BF16)

        rows = pl.ds(c * ROWS, ROWS)
        place_rows = pl.ds(32 * core + c * ROWS, ROWS)
        keep = pltpu.make_async_copy(
            result.at[rows, own_cols, :], o_ref.at[place_rows], out_sems.at[2, c]
        )
        keep.start()
        give = pltpu.make_async_remote_copy(
            src_ref=result.at[rows, away_cols, :], dst_ref=o_ref.at[place_rows],
            send_sem=out_sems.at[0, c], recv_sem=out_sems.at[1, c],
            device_id=sibling, device_id_type=MESH,
        )
        give.start()
        outs += [keep, give]
    wait_all(right_send, 127, right_sems.at[4], right_sems.at[0]).wait_send()
    for c in range(CHUNKS):
        wait_all(left_send.at[c], 127, left_sems.at[0, c], left_sems.at[1, c]).wait_send()
        wait_all(left_send.at[c], 127, tri_sems.at[0, c], tri_sems.at[1, c]).wait_send()
    for out in outs:
        out.wait()


def place_kernel(src_ref, dst_ref, tiles, sems):
    parts = [pl.ds(16 * i, 16) for i in range(4)]
    loads = [
        pltpu.make_async_copy(src_ref.at[part], tiles.at[part], sems.at[0, i])
        for i, part in enumerate(parts)
    ]
    stores = [
        pltpu.make_async_copy(tiles.at[part], dst_ref.at[part], sems.at[1, i])
        for i, part in enumerate(parts)
    ]
    for load in loads:
        load.start()
    for load, store in zip(loads, stores):
        load.wait()
        store.start()
    for store in stores:
        store.wait()


def shards(pair_rep, in_gain, proj_weight, gate_weight, out_gain, out_weight):
    anywhere = pl.BlockSpec(memory_space=pl.ANY)
    update = pl.pallas_call(
        kernel,
        out_shape=jax.ShapeDtypeStruct((64, 64, 128), BF16),
        in_specs=[anywhere] * 6,
        out_specs=anywhere,
        scratch_shapes=[
            pltpu.VMEM((64, 64, 128), BF16),
            pltpu.VMEM((1, 128), F32),
            pltpu.VMEM((128, 512), BF16),
            pltpu.VMEM((128, 128), BF16),
            pltpu.VMEM((1, 128), F32),
            pltpu.VMEM((128, 128), BF16),
            pltpu.VMEM((32, 128, 128), BF16),
            pltpu.VMEM((32, 64, 128), BF16),
            pltpu.VMEM((128 * 32, 128), F32),
            pltpu.VMEM((128, 32, 128), BF16),
            pltpu.VMEM((CHUNKS, 128, ROWS, 128), BF16),
            pltpu.VMEM((16, 2, 8, 32, 128), BF16),
            pltpu.VMEM((CHUNKS, 8, 2, 8, ROWS, 128), BF16),
            pltpu.VMEM((CHUNKS, 8, 2, 8, ROWS, 128), BF16),
            pltpu.VMEM((CHUNKS, 128, ROWS, 128), BF16),
            pltpu.VMEM((32, 128, 128), F32),
            pltpu.VMEM((32, 128, 128), BF16),
            pltpu.VMEM((512, 128), BF16),
            pltpu.VMEM((128, 128), F32),
            pltpu.SemaphoreType.REGULAR,
            pltpu.SemaphoreType.DMA((6,)),
            pltpu.SemaphoreType.DMA((2, 4)),
            pltpu.SemaphoreType.DMA((5,)),
            pltpu.SemaphoreType.DMA((1 + 2 * CHUNKS,)),
            pltpu.SemaphoreType.DMA((2, 4)),
            pltpu.SemaphoreType.DMA((2, CHUNKS)),
            pltpu.SemaphoreType.DMA((2, CHUNKS)),
            pltpu.SemaphoreType.DMA((3, CHUNKS)),
        ],
        compiler_params=pltpu.CompilerParams(
            collective_id=0, has_side_effects=True, vmem_limit_bytes=60 * 2**20
        ),
    )(
        pair_rep, in_gain.reshape(1, 128), proj_weight, gate_weight,
        out_gain.reshape(1, 128), out_weight,
    )
    return pl.pallas_call(
        place_kernel,
        out_shape=jax.ShapeDtypeStruct((64, 64, 128), BF16),
        in_specs=[anywhere],
        out_specs=anywhere,
        scratch_shapes=[
            pltpu.VMEM((64, 64, 128), BF16),
            pltpu.SemaphoreType.DMA((2, 4)),
        ],
        compiler_params=pltpu.CompilerParams(vmem_limit_bytes=60 * 2**20),
    )(update)


def solution(mesh):
    return jax.shard_map(
        shards,
        mesh=mesh,
        in_specs=(P("row", "col", None), P(), P(), P(), P(), P()),
        out_specs=P("row", "col", None),
        check_vma=False,
    )
```
